32 devices in a mesh: groups: 2 (over y), shard: 8 (over z, x), rep: 2 (over core).
Axes of the slice: x: 2, y: 2, z: 4, core: 2. Of those that a mesh axis runs over, the one named last changes fastest.
Arguments:
- queries: bfloat16 [256, 32, 128], P(('groups', 'shard', 'rep')), parts along dimension 0, may hold values from -1.796875 to 1.796875
- passages: bfloat16 [1024, 192, 128], P(('groups', 'shard')), parts along dimension 0, may hold values from -1.796875 to 1.796875
- lengths: int32 [1024], P(('groups', 'shard')), parts along dimension 0, may hold values from 24 to 192
- token_mask: int32 [1024, 192], P(('groups', 'shard')), parts along dimension 0, may hold values 0 or 1
- cand_owner: int32 [256, 100], P(('groups', 'shard', 'rep')), parts along dimension 0, may hold values from 0 to 7, as said below
- cand_slot: int32 [256, 100], P(('groups', 'shard', 'rep')), parts along dimension 0, may hold values from 0 to 63
Outputs:
- scores: float32 [256, 100], P(('groups', 'shard', 'rep')), parts along dimension 0
The draws below stay inside these ranges and needn't reach their ends.
There are 2 independent parts, one for each index of `groups`. The reference program is written for one: setup_inputs(seed, part) draws one part's arguments, and reference() takes and returns one part's arrays. A program takes and returns all parts, laid end to end along the dimension named above; each array names one. Nothing has to cross between parts.
Inputs may be any that keep to these rules, and one draw needn't show every extreme that they name: `cand_owner`: no query names more than 13 candidates of one owner, and some query names exactly 13.
All inputs are finite; a program needn't handle non-finite values. No bound on the sum of `token_mask` on one device may be relied on, other than what follows from the above.
Results may differ from the reference program's by a relative error of at most 0.0003.
Values may be sent and summed in bfloat16 or wider, within the bound.
No kernel may reach another device: no remote copies, remote signals or barrier semaphores. Data moves between devices by JAX's collectives and lax.ppermute only.
A program may use at most 64 MiB of HBM per device.

```python
import jax
import jax.numpy as jnp
from jax import lax

DIM = 128
QT = 32
L_TOK = 192
CAND = 100
P_DEV = 64
QUERIES = 128
PASSAGES = 512
N_SHARD = 8


def draw_cand_owner(key, part):
    key = jax.random.fold_in(key, 7)
    offset_key, ranking_key = jax.random.split(key)
    offset = jax.random.randint(offset_key, (QUERIES, 1), 0, N_SHARD)
    row_keys = jax.random.split(ranking_key, QUERIES)
    ranking = jax.vmap(lambda row_key: jax.random.permutation(row_key, CAND))(row_keys)
    return ((offset + ranking) % N_SHARD).astype(jnp.int32)


def place_ends(result, rng, smallest, top_value):
    dims = result.shape
    spot = [jax.random.randint(jax.random.fold_in(rng, axis), (), 0, dims[axis]) for axis in range(len(dims))]
    result = result.at[tuple(spot)].set(smallest)
    longest = dims.index(max(dims))
    spot[longest] = (spot[longest] + 1) % dims[longest]
    return result.at[tuple(spot)].set(top_value)


def shard_levels(stream_key, extent, cuts, least, high):
    level, own = 1.0, jax.random.fold_in(stream_key, 6)
    for position, parts in cuts:
        draws = jnp.exp(jax.random.uniform(jax.random.fold_in(own, position), (parts,), jnp.float32, least / len(cuts), high / len(cuts)))
        level = level * jnp.repeat(draws, extent[position] // parts).reshape([-1 if axis == position else 1 for axis in range(len(extent))])
    return level


def noise(own_key, shape, deviation, limit, pieces=(), kind=jnp.bfloat16):
    level = shard_levels(own_key, shape, pieces, -0.22, 0.18) if pieces else 1.0
    values = jax.random.normal(own_key, shape, jnp.float32) * deviation * level
    return jnp.minimum(jnp.maximum(values, -limit), limit).astype(kind)


def setup_inputs(seed: int = 0, part: int = 0) -> dict:
    splits = jax.random.split(jax.random.key(seed), 7)
    part_keys = jax.random.split(jax.random.fold_in(splits[6], part), 7)
    queries = noise(part_keys[0], (QUERIES, QT, DIM), 0.3, 1.796875, ((0, 16),))
    passages = noise(part_keys[1], (PASSAGES, L_TOK, DIM), 0.3, 1.796875, ((0, 8),))
    lengths = place_ends(jax.random.randint(part_keys[2], (PASSAGES,), L_TOK // 8, L_TOK + 1), jax.random.fold_in(part_keys[2], 1), L_TOK // 8, L_TOK).astype(jnp.int32)
    token_mask = place_ends((jax.random.randint(part_keys[3], (PASSAGES, L_TOK), 0, 8) < 7).astype(jnp.int32), jax.random.fold_in(part_keys[3], 1), 0, 1)
    cand_owner = draw_cand_owner(jax.random.fold_in(jax.random.fold_in(splits[6], part), 71), part)
    cand_slot = place_ends(jax.random.randint(part_keys[5], (QUERIES, CAND), 0, P_DEV), jax.random.fold_in(part_keys[5], 1), 0, P_DEV - 1).astype(jnp.int32)
    return dict(queries=queries, passages=passages, lengths=lengths, token_mask=token_mask, cand_owner=cand_owner, cand_slot=cand_slot)


def reference(queries, passages, lengths, token_mask, cand_owner, cand_slot):
    positions = jnp.arange(L_TOK, dtype=jnp.int32)
    valid_tok = (positions[None, :] < lengths[:, None]) & ((token_mask == 1) | (positions[None, :] == 0))
    row_ids = (cand_owner * P_DEV + cand_slot).astype(jnp.int32)

    def score_query(block_args):
        query_tok, query_rows = block_args
        passage_tok = jnp.take(passages, query_rows, axis=0).astype(jnp.float32)
        keep_mask = jnp.take(valid_tok, query_rows, axis=0)
        similar = jnp.einsum("td,cpd->ctp", query_tok.astype(jnp.float32), passage_tok)
        best_match = jnp.max(jnp.where(keep_mask[:, None, :], similar, -1e30), axis=2)
        return jnp.mean(best_match, axis=1)

    return lax.map(score_query, (queries, row_ids))
```

```python
import functools

import jax
import jax.numpy as jnp
from jax import lax
from jax.experimental import pallas as pl
from jax.experimental.pallas import tpu as pltpu
from jax.sharding import PartitionSpec as P

NT = (((1,), (1,)), ((), ()))
CHUNK = 4
MASKED = -1e30


def token_bias(lengths, mask):
    slots, tokens = mask.shape
    positions = lax.broadcasted_iota(jnp.int32, (tokens, slots), 0)
    taken = mask.astype(jnp.float32).T > 0.5
    valid = (positions < lengths.reshape(1, slots)) & (taken | (positions == 0))
    bias = jnp.where(valid, 0.0, MASKED)
    return jnp.concatenate([bias, jnp.zeros((tokens, 128 - slots), jnp.float32)], axis=1).astype(jnp.bfloat16)


def best_matches(passages, bias, query_rows, best):
    slots, tokens, _ = passages.shape
    columns = query_rows.shape[0]
    weights = jnp.concatenate([query_rows, jnp.ones((columns, 128), jnp.bfloat16)], axis=1)
    lane = lax.broadcasted_iota(jnp.int32, (tokens, 128), 1)
    for first in range(0, slots, CHUNK):
        rows = [
            jnp.concatenate([passages[p], jnp.where(lane == p, bias, 0).astype(jnp.bfloat16)], axis=1)
            for p in range(first, first + CHUNK)
        ]
        similar = lax.dot_general(jnp.concatenate(rows, axis=0), weights, NT, preferred_element_type=jnp.float32)
        best[first : first + CHUNK] = jnp.max(similar.reshape(CHUNK, tokens // 8, 8, columns), axis=1)


def token_means(best, count, token_count):
    columns = best.shape[1]
    row = lax.broadcasted_iota(jnp.int32, (count, columns), 0)
    column = lax.broadcasted_iota(jnp.int32, (count, columns), 1)
    pick = (row == lax.div(column, token_count)).astype(jnp.bfloat16)
    total = jnp.zeros((count, best.shape[0]), jnp.float32)
    rest = best
    for _ in range(3):
        part = rest.astype(jnp.bfloat16)
        total = total + lax.dot_general(pick, part, NT, preferred_element_type=jnp.float32)
        rest = rest - part.astype(jnp.float32)
    return total * (1.0 / token_count)


def score_kernel(token_count, first, count, passages, lengths, mask, queries, out, best):
    bias = token_bias(lengths[...], mask[...])
    for start in range(first, first + count, 8):
        rows = queries[start * token_count : (start + 8) * token_count, :]
        best_matches(passages, bias, rows, best)
        out[start - first : start - first + 8, :] = token_means(jnp.max(best[...], axis=1), 8, token_count)


def score(passages, lengths, mask, queries, token_count, first, count):
    slots = passages.shape[0]
    return pl.pallas_call(
        functools.partial(score_kernel, token_count, first, count),
        out_shape=jax.ShapeDtypeStruct((count, slots), jnp.float32),
        in_specs=[pl.BlockSpec(memory_space=pltpu.VMEM)] * 4,
        out_specs=pl.BlockSpec(memory_space=pltpu.VMEM),
        scratch_shapes=[pltpu.VMEM((slots, 8, 8 * token_count), jnp.float32)],
        compiler_params=pltpu.CompilerParams(vmem_limit_bytes=16 * 2**20),
        cost_estimate=pl.CostEstimate(
            flops=2 * count * token_count * slots * passages.shape[1] * 256,
            bytes_accessed=passages.size * 2,
            transcendentals=0,
        ),
    )(passages, lengths, mask, queries)


def select_kernel(returned, owner, slot, out):
    owners, _, slots = returned.shape
    count = owner.shape[1]
    pad = ((0, 0), (0, 128 - count))
    own = jnp.concatenate([owner[...], jnp.zeros((owner.shape[0], 128 - count), jnp.int32)], axis=1)
    at = jnp.concatenate([slot[...], jnp.zeros((owner.shape[0], 128 - count), jnp.int32)], axis=1)
    del pad
    total = jnp.zeros(own.shape, jnp.float32)
    for s in range(owners):
        row = jnp.concatenate([returned[s], returned[s]], axis=1)
        total = jnp.where(own == s, jnp.take_along_axis(row, at, axis=1, mode="promise_in_bounds"), total)
    out[...] = total[:, :count]


def select(returned, owner, slot):
    return pl.pallas_call(
        select_kernel,
        out_shape=jax.ShapeDtypeStruct(owner.shape, jnp.float32),
        in_specs=[pl.BlockSpec(memory_space=pltpu.VMEM)] * 3,
        out_specs=pl.BlockSpec(memory_space=pltpu.VMEM),
    )(returned, owner, slot)


def local(queries, passages, lengths, token_mask, cand_owner, cand_slot):
    shard_count = lax.axis_size("shard")
    query_count, token_count, dim = queries.shape
    rows = queries.reshape(query_count * token_count, dim)
    slots = passages.shape[0]
    if shard_count == 8:
        swap = lambda x, d: lax.ppermute(x, "shard", [(i, i ^ d) for i in range(shard_count)])
        far, mid, near = swap(rows, 4), swap(rows, 6), swap(rows, 2)
        line = jnp.concatenate([rows, near, far, mid], axis=0)
        other = swap(line, 1)
        run = functools.partial(score, passages, lengths, token_mask, token_count=token_count)
        own_scores = run(rows, first=0, count=query_count)
        line_scores = run(line, first=query_count, count=3 * query_count)
        other_scores = run(other, first=0, count=4 * query_count)
        by_step = jnp.concatenate([own_scores, line_scores, other_scores], axis=0).reshape(8, query_count, slots)
        me = lax.axis_index("shard")
        order = jnp.array([0, 2, 4, 6, 1, 3, 5, 7])
        place = jnp.argsort(order)
        by_dest = by_step[place[jnp.arange(8) ^ me]]
    else:
        every = lax.all_gather(rows, "shard", axis=0, tiled=True)

        def step(part):
            return score(passages, lengths, token_mask, part, token_count, 0, query_count)

        by_dest = lax.map(step, every.reshape(shard_count, query_count * token_count, dim))
    returned = lax.all_to_all(by_dest, "shard", split_axis=0, concat_axis=0, tiled=True)
    return select(returned, cand_owner, cand_slot)


def solution(mesh):
    in_specs = (
        P(("groups", "shard", "rep"), None, None),
        P(("groups", "shard"), None, None),
        P(("groups", "shard")),
        P(("groups", "shard"), None),
        P(("groups", "shard", "rep"), None),
        P(("groups", "shard", "rep"), None),
    )
    out_specs = P(("groups", "shard", "rep"), None)
    return jax.shard_map(local, mesh=mesh, in_specs=in_specs, out_specs=out_specs, check_vma=False)
```

```python
import functools

import jax
import jax.numpy as jnp
from jax import lax
from jax.experimental import pallas as pl
from jax.experimental.pallas import tpu as pltpu
from jax.sharding import PartitionSpec as P

NT = (((1,), (1,)), ((), ()))
LANES = 128
GROUP = 8
REQUEST_ROWS = 16
EXTRA = 16
VMEM = pl.BlockSpec(memory_space=pltpu.VMEM)
HBM = pl.BlockSpec(memory_space=pltpu.HBM)


def in_hbm(*arrays):
    return [pltpu.with_memory_space_constraint(a, pltpu.HBM) for a in arrays]


def params(mib):
    return pltpu.CompilerParams(vmem_limit_bytes=mib * 2**20)


def wide(values, fill):
    return jnp.concatenate([values, jnp.full((values.shape[0], LANES - values.shape[1]), fill, values.dtype)], axis=1)


def pack_kernel(rows, owner, slot, out, owner_here, slot_here, sems):
    count = rows.shape[0]
    copies = [
        pltpu.make_async_copy(rows, out.at[pl.ds(0, count)], sems.at[0]),
        pltpu.make_async_copy(owner, owner_here, sems.at[1]),
        pltpu.make_async_copy(slot, slot_here, sems.at[2]),
    ]
    for copy in copies:
        copy.start()
    copies[1].wait()
    copies[2].wait()
    named = jnp.concatenate([wide(owner_here[...], -1), wide(slot_here[...], 0)], axis=0)
    out[count:, :] = named.astype(jnp.float32).astype(jnp.bfloat16)
    copies[0].wait()


def pack(rows, owner, slot):
    return pl.pallas_call(
        pack_kernel,
        out_shape=pltpu.VMEM((rows.shape[0] + REQUEST_ROWS, LANES), jnp.bfloat16),
        in_specs=[HBM] * 3,
        out_specs=VMEM,
        scratch_shapes=[
            pltpu.VMEM(owner.shape, jnp.int32),
            pltpu.VMEM(slot.shape, jnp.int32),
            pltpu.SemaphoreType.DMA((3,)),
        ],
        compiler_params=params(4),
    )(*in_hbm(rows, owner, slot))


def fill_kernel(passages, lengths, mask, out, mask_here, lengths_here, sems):
    slots, tokens, _ = passages.shape
    parts = 8
    each = slots // parts
    head = [
        pltpu.make_async_copy(mask, mask_here, sems.at[parts]),
        pltpu.make_async_copy(lengths, lengths_here, sems.at[parts + 1]),
    ]
    copies = [
        pltpu.make_async_copy(passages.at[pl.ds(i * each, each)], out.at[pl.ds(i * each, each)], sems.at[i])
        for i in range(parts)
    ]
    for copy in head + copies:
        copy.start()
    for copy in head:
        copy.wait()
    positions = lax.broadcasted_iota(jnp.int32, (tokens, slots), 0)
    taken = mask_here[...].astype(jnp.float32).T > 0.5
    valid = (positions < lengths_here[...].reshape(1, slots)) & (taken | (positions == 0))
    valid = wide(jnp.where(valid, 1.0, 0.0), 0.0).astype(jnp.bfloat16)
    lane = lax.broadcasted_iota(jnp.int32, (tokens, LANES), 1)
    ones = jnp.ones((LANES, LANES), jnp.bfloat16)
    for i in range(parts):
        copies[i].wait()
        for p in range(i * each, (i + 1) * each):
            one = jnp.where(lane == p, valid, 0).astype(jnp.bfloat16)
            keep = jnp.dot(one, ones, preferred_element_type=jnp.float32) > 0.5
            tok = out[p].astype(jnp.float32)
            out[p] = jnp.where(keep, tok, tok[0:1]).astype(jnp.bfloat16)


def fill(passages, lengths, mask):
    return pl.pallas_call(
        fill_kernel,
        out_shape=pltpu.VMEM(passages.shape, jnp.bfloat16),
        in_specs=[HBM] * 3,
        out_specs=VMEM,
        scratch_shapes=[
            pltpu.VMEM(mask.shape, jnp.int32),
            pltpu.VMEM(lengths.shape, jnp.int32),
            pltpu.SemaphoreType.DMA((10,)),
        ],
        compiler_params=params(16),
        cost_estimate=pl.CostEstimate(flops=0, bytes_accessed=passages.size * 4, transcendentals=0),
    )(*in_hbm(passages, lengths, mask))


def request_tables(blocks, me, block_rows, block_count, tokens, cand_count, slots):
    per_block = REQUEST_ROWS // 2
    queries = block_count * per_block
    target = []
    for b in range(block_count):
        first = b * block_rows + block_rows - REQUEST_ROWS
        request = blocks[first : first + REQUEST_ROWS, :].astype(jnp.float32)
        target.append(jnp.where(request[:per_block] == me, request[per_block:], -1.0))
    target = jnp.concatenate(target, axis=0)
    lane = lax.broadcasted_iota(jnp.int32, (queries, LANES), 1).astype(jnp.float32)
    named = jnp.zeros((queries, LANES), jnp.float32)
    for c in range(cand_count):
        named = jnp.where(target[:, c : c + 1] == lane, 1.0, named)
    row = lax.broadcasted_iota(jnp.int32, (queries, queries), 0)
    column = lax.broadcasted_iota(jnp.int32, (queries, queries), 1)
    earlier = (column < row).astype(jnp.bfloat16)
    rank = jnp.dot(earlier, named.astype(jnp.bfloat16), preferred_element_type=jnp.float32)
    rank = jnp.where(named > 0.5, rank, -1.0)
    number = lax.broadcasted_iota(jnp.int32, (queries, LANES), 0)
    place = lax.div(number, per_block) * block_rows + lax.rem(number, per_block) * tokens
    place = place.astype(jnp.float32)
    lists = [jnp.sum(jnp.where(rank == r, place, 0.0), axis=0, keepdims=True) for r in range(queries)]
    count = jnp.sum(named, axis=0, keepdims=True)
    return rank, jnp.concatenate(lists, axis=0).astype(jnp.int32), count


def overflow_list(count, slots, most):
    capacity = slots * (most - 1)
    later = jnp.maximum(jnp.floor((count + (GROUP - 1)) * (1.0 / GROUP)) - 1.0, 0.0)
    later = jnp.broadcast_to(later, (8, LANES))
    row = lax.broadcasted_iota(jnp.int32, (LANES, LANES), 0)
    column = lax.broadcasted_iota(jnp.int32, (LANES, LANES), 1)
    before = jnp.dot(later.astype(jnp.bfloat16), (row < column).astype(jnp.bfloat16), preferred_element_type=jnp.float32)
    entry = lax.broadcasted_iota(jnp.int32, (capacity, LANES), 0).astype(jnp.float32)
    mine = ((before[0:1] <= entry) & (entry < before[0:1] + later[0:1])).astype(jnp.bfloat16)
    passage = lax.broadcasted_iota(jnp.int32, (8, LANES), 1).astype(jnp.float32)
    kind = lax.broadcasted_iota(jnp.int32, (8, LANES), 0)
    facts = jnp.where(kind == 0, passage, jnp.where(kind == 1, before, later)).astype(jnp.bfloat16)
    found = lax.dot_general(facts, mine, NT, preferred_element_type=jnp.float32)
    total = jnp.sum(later[0:1], axis=1, keepdims=True)
    at = lax.broadcasted_iota(jnp.int32, (1, capacity), 1).astype(jnp.float32)
    group = jnp.clip(at - found[1:2] + 1.0, 1.0, float(most - 1))
    total = jnp.broadcast_to(total, (1, capacity))
    return jnp.concatenate([found[0:1], group, total], axis=0).astype(jnp.int32)


def token_means(best, tokens):
    columns = best.shape[1]
    row = lax.broadcasted_iota(jnp.int32, (GROUP, columns), 0)
    column = lax.broadcasted_iota(jnp.int32, (GROUP, columns), 1)
    pick = (row == lax.div(column, tokens)).astype(jnp.bfloat16)
    total = jnp.zeros((GROUP, best.shape[0]), jnp.float32)
    rest = best
    for _ in range(3):
        part = rest.astype(jnp.bfloat16)
        total = total + lax.dot_general(pick, part, NT, preferred_element_type=jnp.float32)
        rest = rest - part.astype(jnp.float32)
    return total * (1.0 / tokens)


def score_blocks(
    block_rows, block_count, tokens, cand_count, me, passages, blocks,
    best, table, lists_here, lists, extras_here, extras, sems,
):
    slots, length, dim = passages.shape
    queries = block_count * (REQUEST_ROWS // 2)
    most = queries // GROUP
    rank, listed, count = request_tables(blocks, me, block_rows, block_count, tokens, cand_count, slots)
    capacity = slots * (most - 1)
    lists_here[...] = listed
    copies = [pltpu.make_async_copy(lists_here.at[pl.ds(0, GROUP)], lists.at[pl.ds(0, GROUP)], sems.at[0])]
    copies[0].start()
    if most > 1:
        later = pl.ds(GROUP, queries - GROUP)
        copies.append(pltpu.make_async_copy(lists_here.at[later], lists.at[later], sems.at[1]))
        extras_here[0:3, 0:capacity] = overflow_list(count, slots, most)
        copies.append(pltpu.make_async_copy(extras_here, extras, sems.at[2]))
        copies[1].start()
        copies[2].start()
    copies[0].wait()

    def group_best(p, first):
        rows = [blocks[pl.ds(pl.multiple_of(lists[first + k, p], 16), tokens), :] for k in range(GROUP)]
        similar = lax.dot_general(
            passages[p], jnp.concatenate(rows, axis=0), NT, preferred_element_type=jnp.float32
        )
        return jnp.max(similar.reshape(length // 8, 8, GROUP * tokens), axis=0)

    def extra_facts(e):
        live = e < extras[2, 0]
        return jnp.where(live, extras[0, e], -1), extras[0, e], extras[1, e]

    lane = lax.broadcasted_iota(jnp.int32, (GROUP, LANES), 1)
    for p in range(slots):
        best[p] = group_best(p, 0)
    if most > 1:
        for copy in copies[1:]:
            copy.wait()
        facts = [extra_facts(e) for e in range(EXTRA)]
        for e, (_, p, j) in enumerate(facts):
            best[slots + e] = group_best(p, j * GROUP)
    means = token_means(jnp.max(best[...], axis=1), tokens)
    table[0:GROUP, 0:slots] = means[:, 0:slots]
    if most > 1:
        for j in range(1, most):
            total = jnp.zeros((GROUP, LANES), jnp.float32)
            for e, (at, _, its) in enumerate(facts):
                total = jnp.where(lane == jnp.where(its == j, at, -1), means[:, slots + e : slots + e + 1], total)
            table[j * GROUP : (j + 1) * GROUP, :] = total

        def step(i, carry):
            where = [extra_facts(i * EXTRA + u) for u in range(EXTRA)]
            for u, (_, p, j) in enumerate(where):
                best[u] = group_best(p, j * GROUP)
            means = token_means(jnp.max(best[0:EXTRA], axis=1), tokens)
            for u, (at, _, j) in enumerate(where):
                rows = pl.ds(pl.multiple_of(j * GROUP, GROUP), GROUP)
                table[rows, :] = jnp.where(lane == at, means[:, u : u + 1], table[rows, :])
            return carry

        lax.fori_loop(1, lax.div(extras[2, 0] + (EXTRA - 1), EXTRA), step, 0)
    result = jnp.zeros((queries, LANES), jnp.float32)
    for r in range(queries):
        result = jnp.where(rank == r, table[r : r + 1, :], result)
    return result


def score_scratch(slots, tokens, queries):
    return [
        pltpu.VMEM((slots + EXTRA, 8, GROUP * tokens), jnp.float32),
        pltpu.VMEM((queries, LANES), jnp.float32),
        pltpu.VMEM((queries, LANES), jnp.int32),
        pltpu.SMEM((queries, LANES), jnp.int32),
        pltpu.VMEM((8, 256), jnp.int32),
        pltpu.SMEM((8, 256), jnp.int32),
        pltpu.SemaphoreType.DMA((3,)),
    ]


def cost(passages, queries):
    return pl.CostEstimate(
        flops=2 * passages.size * 256 * (queries // 4), bytes_accessed=passages.size * 2, transcendentals=0
    )


def score_kernel(block_rows, block_count, tokens, cand_count, me, passages, blocks, out, *scratch):
    out[...] = score_blocks(
        block_rows, block_count, tokens, cand_count, me[0].astype(jnp.float32), passages, blocks, *scratch
    )


def score(me, passages, blocks, block_rows, block_count, tokens, cand_count):
    queries = block_count * (REQUEST_ROWS // 2)
    return pl.pallas_call(
        functools.partial(score_kernel, block_rows, block_count, tokens, cand_count),
        out_shape=jax.ShapeDtypeStruct((queries, LANES), jnp.float32),
        in_specs=[pl.BlockSpec(memory_space=pltpu.SMEM), VMEM, VMEM],
        out_specs=VMEM,
        scratch_shapes=score_scratch(passages.shape[0], tokens, queries),
        compiler_params=params(16),
        cost_estimate=cost(passages, queries),
    )(me, passages, blocks)


def last_kernel(steps, block_rows, block_count, tokens, cand_count, me, passages, blocks, line, out, *scratch):
    per_block = REQUEST_ROWS // 2
    result = score_blocks(
        block_rows, block_count, tokens, cand_count, me[0].astype(jnp.float32), passages, blocks, *scratch
    )
    for b, step in enumerate(steps):
        rows = slice(b * per_block, (b + 1) * per_block)
        out[jnp.bitwise_xor(me[0], step)] = line[rows, :]
        out[jnp.bitwise_xor(me[0], step + 1)] = result[rows, :]


def score_last(me, passages, blocks, line, steps, block_rows, block_count, tokens, cand_count):
    per_block = REQUEST_ROWS // 2
    return pl.pallas_call(
        functools.partial(last_kernel, steps, block_rows, block_count, tokens, cand_count),
        out_shape=jax.ShapeDtypeStruct((2 * block_count, per_block, LANES), jnp.float32),
        in_specs=[pl.BlockSpec(memory_space=pltpu.SMEM), VMEM, VMEM, VMEM],
        out_specs=VMEM,
        scratch_shapes=score_scratch(passages.shape[0], tokens, block_count * per_block),
        compiler_params=params(16),
        cost_estimate=cost(passages, block_count * per_block),
    )(me, passages, blocks, line)


def select_kernel(returned, owner, slot, out):
    count = owner.shape[1]
    own, at = wide(owner[...], -1), wide(slot[...], 0)
    total = jnp.zeros(own.shape, jnp.float32)
    for s in range(returned.shape[0]):
        total = jnp.where(own == s, jnp.take_along_axis(returned[s], at, axis=1, mode="promise_in_bounds"), total)
    out[...] = total[:, :count]


def select(returned, owner, slot):
    return pl.pallas_call(
        select_kernel,
        out_shape=jax.ShapeDtypeStruct(owner.shape, jnp.float32),
        in_specs=[VMEM] * 3,
        out_specs=VMEM,
        compiler_params=params(4),
    )(returned, owner, slot)


def local(queries, passages, lengths, token_mask, cand_owner, cand_slot):
    shard_count = lax.axis_size("shard")
    query_count, tokens, dim = queries.shape
    cand_count = cand_owner.shape[1]
    block = pack(queries.reshape(query_count * tokens, dim), cand_owner, cand_slot)
    block_rows = block.shape[0]
    filled = fill(passages, lengths, token_mask)
    me = lax.axis_index("shard").reshape(1)
    sizes = dict(block_rows=block_rows, block_count=4, tokens=tokens, cand_count=cand_count)
    if shard_count == 8:
        swap = lambda x, d: lax.ppermute(x, "shard", [(i, i ^ d) for i in range(shard_count)])
        far, mid, near = swap(block, 4), swap(block, 6), swap(block, 2)
        line = jnp.concatenate([block, near, far, mid], axis=0)
        other = swap(line, 1)
        line_scores = score(me, filled, line, **sizes)
        by_home = score_last(me, filled, other, line_scores, steps=(0, 2, 4, 6), **sizes)
    else:
        every = lax.all_gather(block, "shard", axis=0, tiled=True)
        parts = every.reshape(shard_count // 4, 4 * block_rows, dim)
        by_home = lax.map(lambda part: score(me, filled, part, **sizes), parts)
        by_home = by_home.reshape(shard_count, query_count, LANES)
    returned = lax.all_to_all(by_home, "shard", split_axis=0, concat_axis=0, tiled=True)
    return select(returned, cand_owner, cand_slot)


def solution(mesh):
    in_specs = (
        P(("groups", "shard", "rep"), None, None),
        P(("groups", "shard"), None, None),
        P(("groups", "shard")),
        P(("groups", "shard"), None),
        P(("groups", "shard", "rep"), None),
        P(("groups", "shard", "rep"), None),
    )
    out_specs = P(("groups", "shard", "rep"), None)
    return jax.shard_map(local, mesh=mesh, in_specs=in_specs, out_specs=out_specs, check_vma=False)
```

```python
import functools

import jax
import jax.numpy as jnp
from jax import lax
from jax.experimental import pallas as pl
from jax.experimental.pallas import tpu as pltpu
from jax.sharding import PartitionSpec as P

NT = (((1,), (1,)), ((), ()))
LANES = 128
GROUP = 8
REQUEST_ROWS = 16
EXTRA = 12
VMEM = pl.BlockSpec(memory_space=pltpu.VMEM)
HBM = pl.BlockSpec(memory_space=pltpu.HBM)


def in_hbm(*arrays):
    return [pltpu.with_memory_space_constraint(a, pltpu.HBM) for a in arrays]


def params(mib):
    return pltpu.CompilerParams(vmem_limit_bytes=mib * 2**20)


def wide(values, fill):
    return jnp.concatenate([values, jnp.full((values.shape[0], LANES - values.shape[1]), fill, values.dtype)], axis=1)


def pack_kernel(rows, owner, slot, out, owner_here, slot_here, sems):
    count = rows.shape[0]
    copies = [
        pltpu.make_async_copy(rows, out.at[pl.ds(0, count)], sems.at[0]),
        pltpu.make_async_copy(owner, owner_here, sems.at[1]),
        pltpu.make_async_copy(slot, slot_here, sems.at[2]),
    ]
    for copy in copies:
        copy.start()
    copies[1].wait()
    copies[2].wait()
    named = jnp.concatenate([wide(owner_here[...], -1), wide(slot_here[...], 0)], axis=0)
    out[count:, :] = named.astype(jnp.float32).astype(jnp.bfloat16)
    copies[0].wait()


def pack(rows, owner, slot):
    return pl.pallas_call(
        pack_kernel,
        out_shape=pltpu.VMEM((rows.shape[0] + REQUEST_ROWS, LANES), jnp.bfloat16),
        in_specs=[HBM] * 3,
        out_specs=VMEM,
        scratch_shapes=[
            pltpu.VMEM(owner.shape, jnp.int32),
            pltpu.VMEM(slot.shape, jnp.int32),
            pltpu.SemaphoreType.DMA((3,)),
        ],
        compiler_params=params(4),
    )(*in_hbm(rows, owner, slot))


def fill_kernel(passages, lengths, mask, out, mask_here, lengths_here, sems):
    slots, tokens, _ = passages.shape
    parts = 4
    each = slots // parts
    head = [
        pltpu.make_async_copy(mask, mask_here, sems.at[parts]),
        pltpu.make_async_copy(lengths, lengths_here, sems.at[parts + 1]),
    ]
    copies = [
        pltpu.make_async_copy(passages.at[pl.ds(i * each, each)], out.at[pl.ds(i * each, each)], sems.at[i])
        for i in range(parts)
    ]
    for copy in head + copies:
        copy.start()
    for copy in head:
        copy.wait()
    positions = lax.broadcasted_iota(jnp.int32, (tokens, slots), 0)
    taken = mask_here[...].astype(jnp.float32).T > 0.5
    valid = (positions < lengths_here[...].reshape(1, slots)) & (taken | (positions == 0))
    valid = wide(jnp.where(valid, 1.0, 0.0), 0.0)
    for i in range(parts):
        copies[i].wait()
        for p in range(i * each, (i + 1) * each):
            keep = jnp.broadcast_to(valid[:, p : p + 1], (tokens, LANES)).astype(jnp.bfloat16) > 0.5
            tok = out[p]
            out[p] = jnp.where(keep, tok, tok[0:1])


def fill(passages, lengths, mask):
    return pl.pallas_call(
        fill_kernel,
        out_shape=pltpu.VMEM(passages.shape, jnp.bfloat16),
        in_specs=[HBM] * 3,
        out_specs=VMEM,
        scratch_shapes=[
            pltpu.VMEM(mask.shape, jnp.int32),
            pltpu.VMEM(lengths.shape, jnp.int32),
            pltpu.SemaphoreType.DMA((10,)),
        ],
        compiler_params=params(16),
        cost_estimate=pl.CostEstimate(flops=0, bytes_accessed=passages.size * 4, transcendentals=0),
    )(*in_hbm(passages, lengths, mask))


def request_tables(blocks, me, block_rows, block_count, tokens, cand_count, slots):
    per_block = REQUEST_ROWS // 2
    queries = block_count * per_block
    target = []
    for b in range(block_count):
        first = b * block_rows + block_rows - REQUEST_ROWS
        request = blocks[first : first + REQUEST_ROWS, :].astype(jnp.float32)
        target.append(jnp.where(request[:per_block] == me, request[per_block:], -1.0))
    target = jnp.concatenate(target, axis=0)
    lane = lax.broadcasted_iota(jnp.int32, (queries, LANES), 1).astype(jnp.float32)
    named = jnp.zeros((queries, LANES), jnp.float32)
    for c in range(cand_count):
        named = jnp.where(target[:, c : c + 1] == lane, 1.0, named)
    row = lax.broadcasted_iota(jnp.int32, (queries, queries), 0)
    column = lax.broadcasted_iota(jnp.int32, (queries, queries), 1)
    earlier = (column < row).astype(jnp.bfloat16)
    rank = jnp.dot(earlier, named.astype(jnp.bfloat16), preferred_element_type=jnp.float32)
    rank = jnp.where(named > 0.5, rank, -1.0)
    number = lax.broadcasted_iota(jnp.int32, (queries, LANES), 0)
    place = lax.div(number, per_block) * block_rows + lax.rem(number, per_block) * tokens
    place = place.astype(jnp.float32)
    lists = [jnp.sum(jnp.where(rank == r, place, 0.0), axis=0, keepdims=True) for r in range(queries)]
    count = jnp.sum(named, axis=0, keepdims=True)
    return rank, jnp.concatenate(lists, axis=0).astype(jnp.int32), count


def overflow_list(count, slots, most):
    capacity = slots * (most - 1)
    later = jnp.maximum(jnp.floor((count + (GROUP - 1)) * (1.0 / GROUP)) - 1.0, 0.0)
    later = jnp.broadcast_to(later, (8, LANES))
    row = lax.broadcasted_iota(jnp.int32, (LANES, LANES), 0)
    column = lax.broadcasted_iota(jnp.int32, (LANES, LANES), 1)
    before = jnp.dot(later.astype(jnp.bfloat16), (row < column).astype(jnp.bfloat16), preferred_element_type=jnp.float32)
    entry = lax.broadcasted_iota(jnp.int32, (capacity, LANES), 0).astype(jnp.float32)
    mine = ((before[0:1] <= entry) & (entry < before[0:1] + later[0:1])).astype(jnp.bfloat16)
    passage = lax.broadcasted_iota(jnp.int32, (8, LANES), 1).astype(jnp.float32)
    kind = lax.broadcasted_iota(jnp.int32, (8, LANES), 0)
    facts = jnp.where(kind == 0, passage, jnp.where(kind == 1, before, later)).astype(jnp.bfloat16)
    found = lax.dot_general(facts, mine, NT, preferred_element_type=jnp.float32)
    total = jnp.sum(later[0:1], axis=1, keepdims=True)
    at = lax.broadcasted_iota(jnp.int32, (1, capacity), 1).astype(jnp.float32)
    group = jnp.clip(at - found[1:2] + 1.0, 1.0, float(most - 1))
    total = jnp.broadcast_to(total, (1, capacity))
    return jnp.concatenate([found[0:1], group, total], axis=0).astype(jnp.int32)


def token_means(best, tokens):
    columns = best.shape[1]
    row = lax.broadcasted_iota(jnp.int32, (GROUP, columns), 0)
    column = lax.broadcasted_iota(jnp.int32, (GROUP, columns), 1)
    pick = (row == lax.div(column, tokens)).astype(jnp.bfloat16)
    total = jnp.zeros((GROUP, best.shape[0]), jnp.float32)
    rest = best
    for _ in range(3):
        part = rest.astype(jnp.bfloat16)
        total = total + lax.dot_general(pick, part, NT, preferred_element_type=jnp.float32)
        rest = rest - part.astype(jnp.float32)
    return total * (1.0 / tokens)


def score_blocks(
    block_rows, block_count, tokens, cand_count, me, passages, blocks,
    best, table, lists_here, lists, extras_here, extras, sems,
):
    slots, length, dim = passages.shape
    queries = block_count * (REQUEST_ROWS // 2)
    most = queries // GROUP
    rank, listed, count = request_tables(blocks, me, block_rows, block_count, tokens, cand_count, slots)
    capacity = slots * (most - 1)
    lists_here[...] = listed
    copies = [pltpu.make_async_copy(lists_here.at[pl.ds(0, GROUP)], lists.at[pl.ds(0, GROUP)], sems.at[0])]
    copies[0].start()
    if most > 1:
        later = pl.ds(GROUP, queries - GROUP)
        copies.append(pltpu.make_async_copy(lists_here.at[later], lists.at[later], sems.at[1]))
        extras_here[0:3, 0:capacity] = overflow_list(count, slots, most)
        copies.append(pltpu.make_async_copy(extras_here, extras, sems.at[2]))
        copies[1].start()
        copies[2].start()
    copies[0].wait()

    def group_best(p, first):
        rows = [blocks[pl.ds(pl.multiple_of(lists[first + k, p], 16), tokens), :] for k in range(GROUP)]
        similar = lax.dot_general(
            passages[p], jnp.concatenate(rows, axis=0), NT, preferred_element_type=jnp.float32
        )
        return jnp.max(similar.reshape(length // 8, 8, GROUP * tokens), axis=0)

    def extra_facts(e):
        live = e < extras[2, 0]
        return jnp.where(live, extras[0, e], -1), extras[0, e], extras[1, e]

    lane = lax.broadcasted_iota(jnp.int32, (GROUP, LANES), 1)
    for p in range(slots):
        best[p] = group_best(p, 0)
    if most > 1:
        for copy in copies[1:]:
            copy.wait()
        facts = [extra_facts(e) for e in range(EXTRA)]
        for e, (_, p, j) in enumerate(facts):
            best[slots + e] = group_best(p, j * GROUP)
    means = token_means(jnp.max(best[...], axis=1), tokens)
    table[0:GROUP, 0:slots] = means[:, 0:slots]
    if most > 1:
        for j in range(1, most):
            total = jnp.zeros((GROUP, LANES), jnp.float32)
            for e, (at, _, its) in enumerate(facts):
                total = jnp.where(lane == jnp.where(its == j, at, -1), means[:, slots + e : slots + e + 1], total)
            table[j * GROUP : (j + 1) * GROUP, :] = total

        def step(i, carry):
            where = [extra_facts(i * EXTRA + u) for u in range(EXTRA)]
            for u, (_, p, j) in enumerate(where):
                best[u] = group_best(p, j * GROUP)
            means = token_means(jnp.max(best[0:EXTRA], axis=1), tokens)
            for u, (at, _, j) in enumerate(where):
                rows = pl.ds(pl.multiple_of(j * GROUP, GROUP), GROUP)
                table[rows, :] = jnp.where(lane == at, means[:, u : u + 1], table[rows, :])
            return carry

        lax.fori_loop(1, lax.div(extras[2, 0] + (EXTRA - 1), EXTRA), step, 0)
    result = jnp.zeros((queries, LANES), jnp.float32)
    for r in range(queries):
        result = jnp.where(rank == r, table[r : r + 1, :], result)
    return result


def score_scratch(slots, tokens, queries):
    return [
        pltpu.VMEM((slots + EXTRA, 8, GROUP * tokens), jnp.float32),
        pltpu.VMEM((queries, LANES), jnp.float32),
        pltpu.VMEM((queries, LANES), jnp.int32),
        pltpu.SMEM((queries, LANES), jnp.int32),
        pltpu.VMEM((8, 256), jnp.int32),
        pltpu.SMEM((8, 256), jnp.int32),
        pltpu.SemaphoreType.DMA((3,)),
    ]


def cost(passages, queries):
    return pl.CostEstimate(
        flops=2 * passages.size * 256 * (queries // 4), bytes_accessed=passages.size * 2, transcendentals=0
    )


def score_kernel(block_rows, block_count, tokens, cand_count, me, passages, blocks, out, *scratch):
    out[...] = score_blocks(
        block_rows, block_count, tokens, cand_count, me[0].astype(jnp.float32), passages, blocks, *scratch
    )


def score(me, passages, blocks, block_rows, block_count, tokens, cand_count):
    queries = block_count * (REQUEST_ROWS // 2)
    return pl.pallas_call(
        functools.partial(score_kernel, block_rows, block_count, tokens, cand_count),
        out_shape=jax.ShapeDtypeStruct((queries, LANES), jnp.float32),
        in_specs=[pl.BlockSpec(memory_space=pltpu.SMEM), VMEM, VMEM],
        out_specs=VMEM,
        scratch_shapes=score_scratch(passages.shape[0], tokens, queries),
        compiler_params=params(16),
        cost_estimate=cost(passages, queries),
    )(me, passages, blocks)


def last_kernel(steps, block_rows, block_count, tokens, cand_count, me, passages, blocks, line, out, *scratch):
    per_block = REQUEST_ROWS // 2
    result = score_blocks(
        block_rows, block_count, tokens, cand_count, me[0].astype(jnp.float32), passages, blocks, *scratch
    )
    for b, step in enumerate(steps):
        rows = slice(b * per_block, (b + 1) * per_block)
        home = lax.rem(me[0] + (2 * len(steps) - step), 2 * len(steps))
        out[home] = line[rows, :]
        out[jnp.bitwise_xor(home, 1)] = result[rows, :]


def score_last(me, passages, blocks, line, steps, block_rows, block_count, tokens, cand_count):
    per_block = REQUEST_ROWS // 2
    return pl.pallas_call(
        functools.partial(last_kernel, steps, block_rows, block_count, tokens, cand_count),
        out_shape=jax.ShapeDtypeStruct((2 * block_count, per_block, LANES), jnp.float32),
        in_specs=[pl.BlockSpec(memory_space=pltpu.SMEM), VMEM, VMEM, VMEM],
        out_specs=VMEM,
        scratch_shapes=score_scratch(passages.shape[0], tokens, block_count * per_block),
        compiler_params=params(16),
        cost_estimate=cost(passages, block_count * per_block),
    )(me, passages, blocks, line)


def select_kernel(returned, owner, slot, out):
    count = owner.shape[1]
    own, at = wide(owner[...], -1), wide(slot[...], 0)
    total = jnp.zeros(own.shape, jnp.float32)
    for s in range(returned.shape[0]):
        total = jnp.where(own == s, jnp.take_along_axis(returned[s], at, axis=1, mode="promise_in_bounds"), total)
    out[...] = total[:, :count]


def select(returned, owner, slot):
    return pl.pallas_call(
        select_kernel,
        out_shape=jax.ShapeDtypeStruct(owner.shape, jnp.float32),
        in_specs=[VMEM] * 3,
        out_specs=VMEM,
        compiler_params=params(4),
    )(returned, owner, slot)


def local(queries, passages, lengths, token_mask, cand_owner, cand_slot):
    shard_count = lax.axis_size("shard")
    query_count, tokens, dim = queries.shape
    cand_count = cand_owner.shape[1]
    block = pack(queries.reshape(query_count * tokens, dim), cand_owner, cand_slot)
    block_rows = block.shape[0]
    filled = fill(passages, lengths, token_mask)
    me = lax.axis_index("shard").reshape(1)
    sizes = dict(block_rows=block_rows, block_count=4, tokens=tokens, cand_count=cand_count)
    if shard_count == 8:
        swap = lambda x, d: lax.ppermute(x, "shard", [(i, i ^ d) for i in range(shard_count)])
        turn = lambda x, d: lax.ppermute(x, "shard", [(i, (i + d) % shard_count) for i in range(shard_count)])
        near, far, mid = turn(block, 6), turn(block, 4), turn(block, 2)
        own = swap(block, 1)
        near, filled = lax.optimization_barrier((near, filled))
        first = swap(near, 1)
        far, mid, near = lax.optimization_barrier((far, mid, near))
        second = swap(jnp.concatenate([far, mid], axis=0), 1)
        line = jnp.concatenate([block, near, far, mid], axis=0)
        other = jnp.concatenate([own, first, second], axis=0)
        line_scores = score(me, filled, line, **sizes)
        by_home = score_last(me, filled, other, line_scores, steps=(0, 6, 4, 2), **sizes)
    else:
        every = lax.all_gather(block, "shard", axis=0, tiled=True)
        parts = every.reshape(shard_count // 4, 4 * block_rows, dim)
        by_home = lax.map(lambda part: score(me, filled, part, **sizes), parts)
        by_home = by_home.reshape(shard_count, query_count, LANES)
    returned = lax.all_to_all(by_home, "shard", split_axis=0, concat_axis=0, tiled=True)
    return select(returned, cand_owner, cand_slot)


def solution(mesh):
    in_specs = (
        P(("groups", "shard", "rep"), None, None),
        P(("groups", "shard"), None, None),
        P(("groups", "shard")),
        P(("groups", "shard"), None),
        P(("groups", "shard", "rep"), None),
        P(("groups", "shard", "rep"), None),
    )
    out_specs = P(("groups", "shard", "rep"), None)
    return jax.shard_map(local, mesh=mesh, in_specs=in_specs, out_specs=out_specs, check_vma=False)
```

```python
import functools

import jax
import jax.numpy as jnp
from jax import lax
from jax.experimental import pallas as pl
from jax.experimental.pallas import tpu as pltpu
from jax.sharding import PartitionSpec as P

NT = (((1,), (1,)), ((), ()))
LANES = 128
GROUP = 8
REQUEST_ROWS = 16
EARLY = 24
VMEM = pl.BlockSpec(memory_space=pltpu.VMEM)
HBM = pl.BlockSpec(memory_space=pltpu.HBM)


def in_hbm(*arrays):
    return [pltpu.with_memory_space_constraint(a, pltpu.HBM) for a in arrays]


def params(mib):
    return pltpu.CompilerParams(vmem_limit_bytes=mib * 2**20)


def wide(values, fill):
    return jnp.concatenate([values, jnp.full((values.shape[0], LANES - values.shape[1]), fill, values.dtype)], axis=1)


def pack_kernel(rows, owner, slot, out, owner_here, slot_here, sems):
    count = rows.shape[0]
    copies = [
        pltpu.make_async_copy(rows, out.at[pl.ds(0, count)], sems.at[0]),
        pltpu.make_async_copy(owner, owner_here, sems.at[1]),
        pltpu.make_async_copy(slot, slot_here, sems.at[2]),
    ]
    for copy in copies:
        copy.start()
    copies[1].wait()
    copies[2].wait()
    named = jnp.concatenate([wide(owner_here[...], -1), wide(slot_here[...], 0)], axis=0)
    out[count:, :] = named.astype(jnp.float32).astype(jnp.bfloat16)
    copies[0].wait()


def pack(rows, owner, slot):
    return pl.pallas_call(
        pack_kernel,
        out_shape=pltpu.VMEM((rows.shape[0] + REQUEST_ROWS, LANES), jnp.bfloat16),
        in_specs=[HBM] * 3,
        out_specs=VMEM,
        scratch_shapes=[
            pltpu.VMEM(owner.shape, jnp.int32),
            pltpu.VMEM(slot.shape, jnp.int32),
            pltpu.SemaphoreType.DMA((3,)),
        ],
        compiler_params=params(4),
    )(*in_hbm(rows, owner, slot))


def fill_kernel(passages, lengths, mask, out, mask_here, lengths_here, sems):
    slots, tokens, _ = passages.shape
    parts = 4
    each = slots // parts
    head = [
        pltpu.make_async_copy(mask, mask_here, sems.at[parts]),
        pltpu.make_async_copy(lengths, lengths_here, sems.at[parts + 1]),
    ]
    copies = [
        pltpu.make_async_copy(passages.at[pl.ds(i * each, each)], out.at[pl.ds(i * each, each)], sems.at[i])
        for i in range(parts)
    ]
    for copy in head + copies:
        copy.start()
    for copy in head:
        copy.wait()
    positions = lax.broadcasted_iota(jnp.int32, (tokens, slots), 0)
    taken = mask_here[...].astype(jnp.float32).T > 0.5
    valid = (positions < lengths_here[...].reshape(1, slots)) & (taken | (positions == 0))
    valid = wide(jnp.where(valid, 1.0, 0.0), 0.0)
    for i in range(parts):
        copies[i].wait()
        for p in range(i * each, (i + 1) * each):
            keep = jnp.broadcast_to(valid[:, p : p + 1], (tokens, LANES)).astype(jnp.bfloat16) > 0.5
            tok = out[p]
            out[p] = jnp.where(keep, tok, tok[0:1])


def fill(passages, lengths, mask):
    return pl.pallas_call(
        fill_kernel,
        out_shape=pltpu.VMEM(passages.shape, jnp.bfloat16),
        in_specs=[HBM] * 3,
        out_specs=VMEM,
        scratch_shapes=[
            pltpu.VMEM(mask.shape, jnp.int32),
            pltpu.VMEM(lengths.shape, jnp.int32),
            pltpu.SemaphoreType.DMA((10,)),
        ],
        compiler_params=params(16),
        cost_estimate=pl.CostEstimate(flops=0, bytes_accessed=passages.size * 4, transcendentals=0),
    )(*in_hbm(passages, lengths, mask))


def request_tables(blocks, me, block_rows, block_count, tokens, cand_count, slots):
    per_block = REQUEST_ROWS // 2
    queries = block_count * per_block
    target = []
    for b in range(block_count):
        first = b * block_rows + block_rows - REQUEST_ROWS
        request = blocks[first : first + REQUEST_ROWS, :].astype(jnp.float32)
        target.append(jnp.where(request[:per_block] == me, request[per_block:], -1.0))
    target = jnp.concatenate(target, axis=0)
    lane = lax.broadcasted_iota(jnp.int32, (queries, LANES), 1).astype(jnp.float32)
    named = jnp.zeros((queries, LANES), jnp.float32)
    for c in range(cand_count):
        named = jnp.where(target[:, c : c + 1] == lane, 1.0, named)
    row = lax.broadcasted_iota(jnp.int32, (queries, queries), 0)
    column = lax.broadcasted_iota(jnp.int32, (queries, queries), 1)
    earlier = (column < row).astype(jnp.bfloat16)
    rank = jnp.dot(earlier, named.astype(jnp.bfloat16), preferred_element_type=jnp.float32)
    rank = jnp.where(named > 0.5, rank, -1.0)
    number = lax.broadcasted_iota(jnp.int32, (queries, LANES), 0)
    place = lax.div(number, per_block) * block_rows + lax.rem(number, per_block) * tokens
    place = place.astype(jnp.float32)
    lists = [jnp.sum(jnp.where(rank == r, place, 0.0), axis=0, keepdims=True) for r in range(queries)]
    count = jnp.sum(named, axis=0, keepdims=True)
    return rank, jnp.concatenate(lists, axis=0).astype(jnp.int32), count


def overflow_list(count, slots, most):
    capacity = slots * (most - 1)
    later = jnp.maximum(jnp.floor((count + (GROUP - 1)) * (1.0 / GROUP)) - 1.0, 0.0)
    later = jnp.broadcast_to(later, (8, LANES))
    row = lax.broadcasted_iota(jnp.int32, (LANES, LANES), 0)
    column = lax.broadcasted_iota(jnp.int32, (LANES, LANES), 1)
    before = jnp.dot(later.astype(jnp.bfloat16), (row < column).astype(jnp.bfloat16), preferred_element_type=jnp.float32)
    entry = lax.broadcasted_iota(jnp.int32, (capacity, LANES), 0).astype(jnp.float32)
    mine = ((before[0:1] <= entry) & (entry < before[0:1] + later[0:1])).astype(jnp.bfloat16)
    passage = lax.broadcasted_iota(jnp.int32, (8, LANES), 1).astype(jnp.float32)
    kind = lax.broadcasted_iota(jnp.int32, (8, LANES), 0)
    facts = jnp.where(kind == 0, passage, jnp.where(kind == 1, before, later)).astype(jnp.bfloat16)
    found = lax.dot_general(facts, mine, NT, preferred_element_type=jnp.float32)
    total = jnp.sum(later[0:1], axis=1, keepdims=True)
    at = lax.broadcasted_iota(jnp.int32, (1, capacity), 1).astype(jnp.float32)
    group = jnp.clip(at - found[1:2] + 1.0, 1.0, float(most - 1))
    total = jnp.broadcast_to(total, (1, capacity))
    return jnp.concatenate([found[0:1], group, total], axis=0).astype(jnp.int32)


def token_means(best, tokens):
    columns = best.shape[1]
    row = lax.broadcasted_iota(jnp.int32, (GROUP, columns), 0)
    column = lax.broadcasted_iota(jnp.int32, (GROUP, columns), 1)
    pick = (row == lax.div(column, tokens)).astype(jnp.bfloat16)
    total = jnp.zeros((GROUP, best.shape[0]), jnp.float32)
    rest = best
    for _ in range(3):
        part = rest.astype(jnp.bfloat16)
        total = total + lax.dot_general(pick, part, NT, preferred_element_type=jnp.float32)
        rest = rest - part.astype(jnp.float32)
    return total * (1.0 / tokens)


def score_blocks(
    block_rows, block_count, extra, tokens, cand_count, me, passages, blocks,
    best, table, lists_here, lists, extras_here, extras, sems,
):
    slots, length, dim = passages.shape
    queries = block_count * (REQUEST_ROWS // 2)
    most = queries // GROUP
    rank, listed, count = request_tables(blocks, me, block_rows, block_count, tokens, cand_count, slots)
    capacity = slots * (most - 1)
    lists_here[...] = listed
    copies = [pltpu.make_async_copy(lists_here.at[pl.ds(0, GROUP)], lists.at[pl.ds(0, GROUP)], sems.at[0])]
    copies[0].start()
    if most > 1:
        later = pl.ds(GROUP, queries - GROUP)
        copies.append(pltpu.make_async_copy(lists_here.at[later], lists.at[later], sems.at[1]))
        extras_here[0:3, 0:capacity] = overflow_list(count, slots, most)
        copies.append(pltpu.make_async_copy(extras_here, extras, sems.at[2]))
        copies[1].start()
        copies[2].start()
    copies[0].wait()

    def group_best(p, first):
        rows = [blocks[pl.ds(pl.multiple_of(lists[first + k, p], 16), tokens), :] for k in range(GROUP)]
        similar = lax.dot_general(
            passages[p], jnp.concatenate(rows, axis=0), NT, preferred_element_type=jnp.float32
        )
        return jnp.max(similar.reshape(length // 8, 8, GROUP * tokens), axis=0)

    def extra_facts(e):
        live = e < extras[2, 0]
        return jnp.where(live, extras[0, e], -1), extras[0, e], extras[1, e]

    lane = lax.broadcasted_iota(jnp.int32, (GROUP, LANES), 1)
    for p in range(slots):
        if p == EARLY:
            for copy in copies[1:]:
                copy.wait()
        best[p] = group_best(p, 0)
    if most > 1:
        facts = [extra_facts(e) for e in range(extra)]
        for e, (_, p, j) in enumerate(facts):
            best[slots + e] = group_best(p, j * GROUP)
    table[0:GROUP, 0:slots] = token_means(jnp.max(best[0:slots], axis=1), tokens)
    means = token_means(jnp.max(best[slots:], axis=1), tokens)
    if most > 1:
        for j in range(1, most):
            total = jnp.zeros((GROUP, LANES), jnp.float32)
            for e, (at, _, its) in enumerate(facts):
                total = jnp.where(lane == jnp.where(its == j, at, -1), means[:, e : e + 1], total)
            table[j * GROUP : (j + 1) * GROUP, :] = total

        def step(i, carry):
            where = [extra_facts(i * extra + u) for u in range(extra)]
            for u, (_, p, j) in enumerate(where):
                best[u] = group_best(p, j * GROUP)
            means = token_means(jnp.max(best[0:extra], axis=1), tokens)
            for u, (at, _, j) in enumerate(where):
                rows = pl.ds(pl.multiple_of(j * GROUP, GROUP), GROUP)
                table[rows, :] = jnp.where(lane == at, means[:, u : u + 1], table[rows, :])
            return carry

        lax.fori_loop(1, lax.div(extras[2, 0] + (extra - 1), extra), step, 0)
    result = jnp.zeros((queries, LANES), jnp.float32)
    for r in range(queries):
        result = jnp.where(rank == r, table[r : r + 1, :], result)
    return result


def score_scratch(slots, tokens, queries, extra):
    return [
        pltpu.VMEM((slots + extra, 8, GROUP * tokens), jnp.float32),
        pltpu.VMEM((queries, LANES), jnp.float32),
        pltpu.VMEM((queries, LANES), jnp.int32),
        pltpu.SMEM((queries, LANES), jnp.int32),
        pltpu.VMEM((8, 256), jnp.int32),
        pltpu.SMEM((8, 256), jnp.int32),
        pltpu.SemaphoreType.DMA((3,)),
    ]


def cost(passages, queries):
    return pl.CostEstimate(
        flops=2 * passages.size * 256 * (queries // 4), bytes_accessed=passages.size * 2, transcendentals=0
    )


def score_kernel(block_rows, block_count, extra, tokens, cand_count, me, passages, blocks, out, *scratch):
    out[...] = score_blocks(
        block_rows, block_count, extra, tokens, cand_count, me[0].astype(jnp.float32), passages, blocks, *scratch
    )


def score(me, passages, blocks, block_rows, block_count, extra, tokens, cand_count):
    queries = block_count * (REQUEST_ROWS // 2)
    return pl.pallas_call(
        functools.partial(score_kernel, block_rows, block_count, extra, tokens, cand_count),
        out_shape=jax.ShapeDtypeStruct((queries, LANES), jnp.float32),
        in_specs=[pl.BlockSpec(memory_space=pltpu.SMEM), VMEM, VMEM],
        out_specs=VMEM,
        scratch_shapes=score_scratch(passages.shape[0], tokens, queries, extra),
        compiler_params=params(16),
        cost_estimate=cost(passages, queries),
    )(me, passages, blocks)


def last_kernel(
    homes, block_rows, block_count, extra, tokens, cand_count, me, passages, blocks, earlier, out, *scratch
):
    per_block = REQUEST_ROWS // 2
    result = score_blocks(
        block_rows, block_count, extra, tokens, cand_count, me[0].astype(jnp.float32), passages, blocks, *scratch
    )
    before = len(homes) - block_count
    for b, (step, side) in enumerate(homes):
        home = jnp.bitwise_xor(lax.rem(me[0] + (len(homes) - step), len(homes)), side)
        at = (b if b < before else b - before) * per_block
        out[home] = earlier[at : at + per_block, :] if b < before else result[at : at + per_block, :]


def score_last(me, passages, blocks, earlier, homes, block_rows, block_count, extra, tokens, cand_count):
    per_block = REQUEST_ROWS // 2
    return pl.pallas_call(
        functools.partial(last_kernel, homes, block_rows, block_count, extra, tokens, cand_count),
        out_shape=jax.ShapeDtypeStruct((len(homes), per_block, LANES), jnp.float32),
        in_specs=[pl.BlockSpec(memory_space=pltpu.SMEM), VMEM, VMEM, VMEM],
        out_specs=VMEM,
        scratch_shapes=score_scratch(passages.shape[0], tokens, block_count * per_block, extra),
        compiler_params=params(16),
        cost_estimate=cost(passages, block_count * per_block),
    )(me, passages, blocks, earlier)


def select_kernel(returned, owner, slot, out):
    count = owner.shape[1]
    own, at = wide(owner[...], -1), wide(slot[...], 0)
    total = jnp.zeros(own.shape, jnp.float32)
    for s in range(returned.shape[0]):
        total = jnp.where(own == s, jnp.take_along_axis(returned[s], at, axis=1, mode="promise_in_bounds"), total)
    out[...] = total[:, :count]


def select(returned, owner, slot):
    return pl.pallas_call(
        select_kernel,
        out_shape=jax.ShapeDtypeStruct(owner.shape, jnp.float32),
        in_specs=[VMEM] * 3,
        out_specs=VMEM,
        compiler_params=params(4),
    )(returned, owner, slot)


def local(queries, passages, lengths, token_mask, cand_owner, cand_slot):
    shard_count = lax.axis_size("shard")
    query_count, tokens, dim = queries.shape
    cand_count = cand_owner.shape[1]
    block = pack(queries.reshape(query_count * tokens, dim), cand_owner, cand_slot)
    block_rows = block.shape[0]
    filled = fill(passages, lengths, token_mask)
    me = lax.axis_index("shard").reshape(1)
    sizes = dict(block_rows=block_rows, tokens=tokens, cand_count=cand_count)
    if shard_count == 8:
        swap = lambda x, d: lax.ppermute(x, "shard", [(i, i ^ d) for i in range(shard_count)])
        turn = lambda x, d: lax.ppermute(x, "shard", [(i, (i + d) % shard_count) for i in range(shard_count)])
        near, far, mid = turn(block, 6), turn(block, 4), turn(block, 2)
        own = swap(block, 1)
        near, filled = lax.optimization_barrier((near, filled))
        first = swap(near, 1)
        far, mid, near = lax.optimization_barrier((far, mid, near))
        second = swap(jnp.concatenate([far, mid], axis=0), 1)
        early = jnp.concatenate([block, near, far, mid, own], axis=0)
        late = jnp.concatenate([first, second], axis=0)
        early_scores = score(me, filled, early, block_count=5, extra=24, **sizes)
        homes = ((0, 0), (6, 0), (4, 0), (2, 0), (0, 1), (6, 1), (4, 1), (2, 1))
        by_home = score_last(me, filled, late, early_scores, homes, block_count=3, extra=4, **sizes)
    else:
        every = lax.all_gather(block, "shard", axis=0, tiled=True)
        parts = every.reshape(shard_count // 4, 4 * block_rows, dim)
        by_home = lax.map(lambda part: score(me, filled, part, block_count=4, extra=12, **sizes), parts)
        by_home = by_home.reshape(shard_count, query_count, LANES)
    returned = lax.all_to_all(by_home, "shard", split_axis=0, concat_axis=0, tiled=True)
    return select(returned, cand_owner, cand_slot)


def solution(mesh):
    in_specs = (
        P(("groups", "shard", "rep"), None, None),
        P(("groups", "shard"), None, None),
        P(("groups", "shard")),
        P(("groups", "shard"), None),
        P(("groups", "shard", "rep"), None),
        P(("groups", "shard", "rep"), None),
    )
    out_specs = P(("groups", "shard", "rep"), None)
    return jax.shard_map(local, mesh=mesh, in_specs=in_specs, out_specs=out_specs, check_vma=False)
```

```python
import functools

import jax
import jax.numpy as jnp
from jax import lax
from jax.experimental import pallas as pl
from jax.experimental.pallas import tpu as pltpu
from jax.sharding import PartitionSpec as P

NT = (((1,), (1,)), ((), ()))
LANES = 128
GROUP = 8
REQUEST_ROWS = 16
EARLY = 24
VMEM = pl.BlockSpec(memory_space=pltpu.VMEM)
HBM = pl.BlockSpec(memory_space=pltpu.HBM)


def in_hbm(*arrays):
    return [pltpu.with_memory_space_constraint(a, pltpu.HBM) for a in arrays]


def params(mib):
    return pltpu.CompilerParams(vmem_limit_bytes=mib * 2**20)


def wide(values, fill):
    return jnp.concatenate([values, jnp.full((values.shape[0], LANES - values.shape[1]), fill, values.dtype)], axis=1)


def pack_kernel(rows, owner, slot, out, owner_here, slot_here, sems):
    count = rows.shape[0]
    copies = [
        pltpu.make_async_copy(rows.at[pl.ds(0, count // 2)], out.at[pl.ds(0, count // 2)], sems.at[0]),
        pltpu.make_async_copy(owner, owner_here, sems.at[1]),
        pltpu.make_async_copy(slot, slot_here, sems.at[2]),
        pltpu.make_async_copy(rows.at[pl.ds(count // 2, count // 2)], out.at[pl.ds(count // 2, count // 2)], sems.at[3]),
    ]
    for copy in copies:
        copy.start()
    copies[1].wait()
    copies[2].wait()
    named = jnp.concatenate([wide(owner_here[...], -1), wide(slot_here[...], 0)], axis=0)
    out[count:, :] = named.astype(jnp.float32).astype(jnp.bfloat16)
    copies[0].wait()
    copies[3].wait()


def pack(rows, owner, slot):
    return pl.pallas_call(
        pack_kernel,
        out_shape=pltpu.VMEM((rows.shape[0] + REQUEST_ROWS, LANES), jnp.bfloat16),
        in_specs=[HBM] * 3,
        out_specs=VMEM,
        scratch_shapes=[
            pltpu.VMEM(owner.shape, jnp.int32),
            pltpu.VMEM(slot.shape, jnp.int32),
            pltpu.SemaphoreType.DMA((4,)),
        ],
        compiler_params=params(4),
    )(*in_hbm(rows, owner, slot))


def fill_kernel(passages, lengths, mask, out, mask_here, lengths_here, sems):
    slots, tokens, _ = passages.shape
    parts = 4
    each = slots // parts
    head = [
        pltpu.make_async_copy(mask, mask_here, sems.at[parts]),
        pltpu.make_async_copy(lengths, lengths_here, sems.at[parts + 1]),
    ]
    copies = [
        pltpu.make_async_copy(passages.at[pl.ds(i * each, each)], out.at[pl.ds(i * each, each)], sems.at[i])
        for i in range(parts)
    ]
    for copy in head + copies:
        copy.start()
    for copy in head:
        copy.wait()
    positions = lax.broadcasted_iota(jnp.int32, (tokens, slots), 0)
    taken = mask_here[...].astype(jnp.float32).T > 0.5
    valid = (positions < lengths_here[...].reshape(1, slots)) & (taken | (positions == 0))
    valid = wide(jnp.where(valid, 1.0, 0.0), 0.0)
    for i in range(parts):
        copies[i].wait()
        for p in range(i * each, (i + 1) * each):
            keep = jnp.broadcast_to(valid[:, p : p + 1], (tokens, LANES)).astype(jnp.bfloat16) > 0.5
            tok = out[p]
            out[p] = jnp.where(keep, tok, tok[0:1])


def fill(passages, lengths, mask):
    return pl.pallas_call(
        fill_kernel,
        out_shape=pltpu.VMEM(passages.shape, jnp.bfloat16),
        in_specs=[HBM] * 3,
        out_specs=VMEM,
        scratch_shapes=[
            pltpu.VMEM(mask.shape, jnp.int32),
            pltpu.VMEM(lengths.shape, jnp.int32),
            pltpu.SemaphoreType.DMA((10,)),
        ],
        compiler_params=params(16),
        cost_estimate=pl.CostEstimate(flops=0, bytes_accessed=passages.size * 4, transcendentals=0),
    )(*in_hbm(passages, lengths, mask))


def request_tables(blocks, me, block_rows, block_count, tokens, cand_count, slots):
    per_block = REQUEST_ROWS // 2
    queries = block_count * per_block
    target = []
    for b in range(block_count):
        first = b * block_rows + block_rows - REQUEST_ROWS
        request = blocks[first : first + REQUEST_ROWS, :].astype(jnp.float32)
        target.append(jnp.where(request[:per_block] == me, request[per_block:], -1.0))
    target = jnp.concatenate(target, axis=0)
    lane = lax.broadcasted_iota(jnp.int32, (queries, LANES), 1).astype(jnp.float32)
    named = jnp.zeros((queries, LANES), jnp.float32)
    for c in range(cand_count):
        named = jnp.where(target[:, c : c + 1] == lane, 1.0, named)
    row = lax.broadcasted_iota(jnp.int32, (queries, queries), 0)
    column = lax.broadcasted_iota(jnp.int32, (queries, queries), 1)
    earlier = (column < row).astype(jnp.bfloat16)
    rank = jnp.dot(earlier, named.astype(jnp.bfloat16), preferred_element_type=jnp.float32)
    rank = jnp.where(named > 0.5, rank, -1.0)
    number = lax.broadcasted_iota(jnp.int32, (queries, LANES), 0)
    place = lax.div(number, per_block) * block_rows + lax.rem(number, per_block) * tokens
    place = place.astype(jnp.float32)
    count = jnp.sum(named, axis=0, keepdims=True)
    return rank, place, count


def list_rows(rank, place, first, last):
    rows = [jnp.sum(jnp.where(rank == r, place, 0.0), axis=0, keepdims=True) for r in range(first, last)]
    return jnp.concatenate(rows, axis=0).astype(jnp.int32)


def overflow_list(count, slots, most):
    capacity = slots * (most - 1)
    later = jnp.maximum(jnp.floor((count + (GROUP - 1)) * (1.0 / GROUP)) - 1.0, 0.0)
    later = jnp.broadcast_to(later, (8, LANES))
    row = lax.broadcasted_iota(jnp.int32, (LANES, LANES), 0)
    column = lax.broadcasted_iota(jnp.int32, (LANES, LANES), 1)
    before = jnp.dot(later.astype(jnp.bfloat16), (row < column).astype(jnp.bfloat16), preferred_element_type=jnp.float32)
    entry = lax.broadcasted_iota(jnp.int32, (capacity, LANES), 0).astype(jnp.float32)
    mine = ((before[0:1] <= entry) & (entry < before[0:1] + later[0:1])).astype(jnp.bfloat16)
    passage = lax.broadcasted_iota(jnp.int32, (8, LANES), 1).astype(jnp.float32)
    kind = lax.broadcasted_iota(jnp.int32, (8, LANES), 0)
    facts = jnp.where(kind == 0, passage, jnp.where(kind == 1, before, later)).astype(jnp.bfloat16)
    found = lax.dot_general(facts, mine, NT, preferred_element_type=jnp.float32)
    total = jnp.sum(later[0:1], axis=1, keepdims=True)
    at = lax.broadcasted_iota(jnp.int32, (1, capacity), 1).astype(jnp.float32)
    group = jnp.clip(at - found[1:2] + 1.0, 1.0, float(most - 1))
    total = jnp.broadcast_to(total, (1, capacity))
    return jnp.concatenate([found[0:1], group, total], axis=0).astype(jnp.int32)


def token_means(best, tokens):
    columns = best.shape[1]
    row = lax.broadcasted_iota(jnp.int32, (GROUP, columns), 0)
    column = lax.broadcasted_iota(jnp.int32, (GROUP, columns), 1)
    pick = (row == lax.div(column, tokens)).astype(jnp.bfloat16)
    total = jnp.zeros((GROUP, best.shape[0]), jnp.float32)
    rest = best
    for _ in range(3):
        part = rest.astype(jnp.bfloat16)
        total = total + lax.dot_general(pick, part, NT, preferred_element_type=jnp.float32)
        rest = rest - part.astype(jnp.float32)
    return total * (1.0 / tokens)


def score_blocks(
    block_rows, block_count, extra, tokens, cand_count, me, passages, blocks,
    best, table, lists_here, lists, extras_here, extras, sems,
):
    slots, length, dim = passages.shape
    queries = block_count * (REQUEST_ROWS // 2)
    most = queries // GROUP
    rank, place, count = request_tables(blocks, me, block_rows, block_count, tokens, cand_count, slots)
    capacity = slots * (most - 1)
    lists_here[0:GROUP, :] = list_rows(rank, place, 0, GROUP)
    copies = [pltpu.make_async_copy(lists_here.at[pl.ds(0, GROUP)], lists.at[pl.ds(0, GROUP)], sems.at[0])]
    copies[0].start()
    if most > 1:
        lists_here[GROUP:, :] = list_rows(rank, place, GROUP, queries)
        later = pl.ds(GROUP, queries - GROUP)
        copies.append(pltpu.make_async_copy(lists_here.at[later], lists.at[later], sems.at[1]))
        extras_here[0:3, 0:capacity] = overflow_list(count, slots, most)
        copies.append(pltpu.make_async_copy(extras_here, extras, sems.at[2]))
        copies[1].start()
        copies[2].start()
    copies[0].wait()

    def group_best(p, first):
        rows = [blocks[pl.ds(pl.multiple_of(lists[first + k, p], 16), tokens), :] for k in range(GROUP)]
        similar = lax.dot_general(
            passages[p], jnp.concatenate(rows, axis=0), NT, preferred_element_type=jnp.float32
        )
        return jnp.max(similar.reshape(length // 8, 8, GROUP * tokens), axis=0)

    def extra_facts(e):
        live = e < extras[2, 0]
        return jnp.where(live, extras[0, e], -1), extras[0, e], extras[1, e]

    lane = lax.broadcasted_iota(jnp.int32, (GROUP, LANES), 1)
    for p in range(slots):
        if p == EARLY:
            for copy in copies[1:]:
                copy.wait()
        best[p] = group_best(p, 0)
    if most > 1:
        facts = [extra_facts(e) for e in range(extra)]
        for e, (_, p, j) in enumerate(facts):
            best[slots + e] = group_best(p, j * GROUP)
    table[0:GROUP, 0:slots] = token_means(jnp.max(best[0:slots], axis=1), tokens)
    means = token_means(jnp.max(best[slots:], axis=1), tokens)
    if most > 1:
        for j in range(1, most):
            total = jnp.zeros((GROUP, LANES), jnp.float32)
            for e, (at, _, its) in enumerate(facts):
                total = jnp.where(lane == jnp.where(its == j, at, -1), means[:, e : e + 1], total)
            table[j * GROUP : (j + 1) * GROUP, :] = total

        def step(i, carry):
            where = [extra_facts(i * extra + u) for u in range(extra)]
            for u, (_, p, j) in enumerate(where):
                best[u] = group_best(p, j * GROUP)
            means = token_means(jnp.max(best[0:extra], axis=1), tokens)
            for u, (at, _, j) in enumerate(where):
                rows = pl.ds(pl.multiple_of(j * GROUP, GROUP), GROUP)
                table[rows, :] = jnp.where(lane == at, means[:, u : u + 1], table[rows, :])
            return carry

        lax.fori_loop(1, lax.div(extras[2, 0] + (extra - 1), extra), step, 0)
    result = jnp.zeros((queries, LANES), jnp.float32)
    for r in range(queries):
        result = jnp.where(rank == r, table[r : r + 1, :], result)
    return result


def score_scratch(slots, tokens, queries, extra):
    return [
        pltpu.VMEM((slots + extra, 8, GROUP * tokens), jnp.float32),
        pltpu.VMEM((queries, LANES), jnp.float32),
        pltpu.VMEM((queries, LANES), jnp.int32),
        pltpu.SMEM((queries, LANES), jnp.int32),
        pltpu.VMEM((8, 256), jnp.int32),
        pltpu.SMEM((8, 256), jnp.int32),
        pltpu.SemaphoreType.DMA((3,)),
    ]


def cost(passages, queries):
    return pl.CostEstimate(
        flops=2 * passages.size * 256 * (queries // 4), bytes_accessed=passages.size * 2, transcendentals=0
    )


def score_kernel(block_rows, block_count, extra, tokens, cand_count, me, passages, blocks, out, *scratch):
    out[...] = score_blocks(
        block_rows, block_count, extra, tokens, cand_count, me[0].astype(jnp.float32), passages, blocks, *scratch
    )


def score(me, passages, blocks, block_rows, block_count, extra, tokens, cand_count):
    queries = block_count * (REQUEST_ROWS // 2)
    return pl.pallas_call(
        functools.partial(score_kernel, block_rows, block_count, extra, tokens, cand_count),
        out_shape=jax.ShapeDtypeStruct((queries, LANES), jnp.float32),
        in_specs=[pl.BlockSpec(memory_space=pltpu.SMEM), VMEM, VMEM],
        out_specs=VMEM,
        scratch_shapes=score_scratch(passages.shape[0], tokens, queries, extra),
        compiler_params=params(16),
        cost_estimate=cost(passages, queries),
    )(me, passages, blocks)


def last_kernel(
    homes, block_rows, block_count, extra, tokens, cand_count, me, passages, blocks, earlier, out, *scratch
):
    per_block = REQUEST_ROWS // 2
    result = score_blocks(
        block_rows, block_count, extra, tokens, cand_count, me[0].astype(jnp.float32), passages, blocks, *scratch
    )
    before = len(homes) - block_count
    for b, (step, side) in enumerate(homes):
        home = jnp.bitwise_xor(lax.rem(me[0] + (len(homes) - step), len(homes)), side)
        at = (b if b < before else b - before) * per_block
        out[home] = earlier[at : at + per_block, :] if b < before else result[at : at + per_block, :]


def score_last(me, passages, blocks, earlier, homes, block_rows, block_count, extra, tokens, cand_count):
    per_block = REQUEST_ROWS // 2
    return pl.pallas_call(
        functools.partial(last_kernel, homes, block_rows, block_count, extra, tokens, cand_count),
        out_shape=jax.ShapeDtypeStruct((len(homes), per_block, LANES), jnp.float32),
        in_specs=[pl.BlockSpec(memory_space=pltpu.SMEM), VMEM, VMEM, VMEM],
        out_specs=VMEM,
        scratch_shapes=score_scratch(passages.shape[0], tokens, block_count * per_block, extra),
        compiler_params=params(16),
        cost_estimate=cost(passages, block_count * per_block),
    )(me, passages, blocks, earlier)


def select_kernel(returned, owner, slot, out):
    count = owner.shape[1]
    own, at = wide(owner[...], -1), wide(slot[...], 0)
    total = jnp.zeros(own.shape, jnp.float32)
    for s in range(returned.shape[0]):
        total = jnp.where(own == s, jnp.take_along_axis(returned[s], at, axis=1, mode="promise_in_bounds"), total)
    out[...] = total[:, :count]


def select(returned, owner, slot):
    return pl.pallas_call(
        select_kernel,
        out_shape=jax.ShapeDtypeStruct(owner.shape, jnp.float32),
        in_specs=[VMEM] * 3,
        out_specs=VMEM,
        compiler_params=params(4),
    )(returned, owner, slot)


def local(queries, passages, lengths, token_mask, cand_owner, cand_slot):
    shard_count = lax.axis_size("shard")
    query_count, tokens, dim = queries.shape
    cand_count = cand_owner.shape[1]
    block = pack(queries.reshape(query_count * tokens, dim), cand_owner, cand_slot)
    block_rows = block.shape[0]
    filled = fill(passages, lengths, token_mask)
    me = lax.axis_index("shard").reshape(1)
    sizes = dict(block_rows=block_rows, tokens=tokens, cand_count=cand_count)
    if shard_count == 8:
        swap = lambda x, d: lax.ppermute(x, "shard", [(i, i ^ d) for i in range(shard_count)])
        turn = lambda x, d: lax.ppermute(x, "shard", [(i, (i + d) % shard_count) for i in range(shard_count)])
        near, far, mid = turn(block, 6), turn(block, 4), turn(block, 2)
        own = swap(block, 1)
        near, filled = lax.optimization_barrier((near, filled))
        first = swap(near, 1)
        far, mid, near = lax.optimization_barrier((far, mid, near))
        second = swap(jnp.concatenate([far, mid], axis=0), 1)
        early = jnp.concatenate([block, near, far, mid, own], axis=0)
        late = jnp.concatenate([first, second], axis=0)
        early_scores = score(me, filled, early, block_count=5, extra=24, **sizes)
        homes = ((0, 0), (6, 0), (4, 0), (2, 0), (0, 1), (6, 1), (4, 1), (2, 1))
        by_home = score_last(me, filled, late, early_scores, homes, block_count=3, extra=4, **sizes)
    else:
        every = lax.all_gather(block, "shard", axis=0, tiled=True)
        parts = every.reshape(shard_count // 4, 4 * block_rows, dim)
        by_home = lax.map(lambda part: score(me, filled, part, block_count=4, extra=12, **sizes), parts)
        by_home = by_home.reshape(shard_count, query_count, LANES)
    returned = lax.all_to_all(by_home, "shard", split_axis=0, concat_axis=0, tiled=True)
    return select(returned, cand_owner, cand_slot)


def solution(mesh):
    in_specs = (
        P(("groups", "shard", "rep"), None, None),
        P(("groups", "shard"), None, None),
        P(("groups", "shard")),
        P(("groups", "shard"), None),
        P(("groups", "shard", "rep"), None),
        P(("groups", "shard", "rep"), None),
    )
    out_specs = P(("groups", "shard", "rep"), None)
    return jax.shard_map(local, mesh=mesh, in_specs=in_specs, out_specs=out_specs, check_vma=False)
```

```python
import functools

import jax
import jax.numpy as jnp
from jax import lax
from jax.experimental import pallas as pl
from jax.experimental.pallas import tpu as pltpu
from jax.sharding import PartitionSpec as P

NT = (((1,), (1,)), ((), ()))
LANES = 128
GROUP = 8
REQUEST_ROWS = 16
EARLY = 24
VMEM = pl.BlockSpec(memory_space=pltpu.VMEM)
HBM = pl.BlockSpec(memory_space=pltpu.HBM)


def in_hbm(*arrays):
    return [pltpu.with_memory_space_constraint(a, pltpu.HBM) for a in arrays]


def params(mib):
    return pltpu.CompilerParams(vmem_limit_bytes=mib * 2**20)


def wide(values, fill):
    return jnp.concatenate([values, jnp.full((values.shape[0], LANES - values.shape[1]), fill, values.dtype)], axis=1)


def pack_kernel(rows, owner, slot, out, owner_here, slot_here, sems):
    count = rows.shape[0]
    copies = [
        pltpu.make_async_copy(rows, out.at[pl.ds(0, count)], sems.at[0]),
        pltpu.make_async_copy(owner, owner_here, sems.at[1]),
        pltpu.make_async_copy(slot, slot_here, sems.at[2]),
    ]
    for copy in copies:
        copy.start()
    copies[1].wait()
    copies[2].wait()
    named = jnp.concatenate([wide(owner_here[...], -1), wide(slot_here[...], 0)], axis=0)
    out[count:, :] = named.astype(jnp.float32).astype(jnp.bfloat16)
    copies[0].wait()


def pack(rows, owner, slot):
    return pl.pallas_call(
        pack_kernel,
        out_shape=pltpu.VMEM((rows.shape[0] + REQUEST_ROWS, LANES), jnp.bfloat16),
        in_specs=[HBM] * 3,
        out_specs=VMEM,
        scratch_shapes=[
            pltpu.VMEM(owner.shape, jnp.int32),
            pltpu.VMEM(slot.shape, jnp.int32),
            pltpu.SemaphoreType.DMA((3,)),
        ],
        compiler_params=params(4),
    )(*in_hbm(rows, owner, slot))


def fill_kernel(passages, lengths, mask, out, mask_here, lengths_here, sems):
    slots, tokens, _ = passages.shape
    parts = 4
    each = slots // parts
    head = [
        pltpu.make_async_copy(mask, mask_here, sems.at[parts]),
        pltpu.make_async_copy(lengths, lengths_here, sems.at[parts + 1]),
    ]
    copies = [
        pltpu.make_async_copy(passages.at[pl.ds(i * each, each)], out.at[pl.ds(i * each, each)], sems.at[i])
        for i in range(parts)
    ]
    for copy in head + copies:
        copy.start()
    for copy in head:
        copy.wait()
    positions = lax.broadcasted_iota(jnp.int32, (tokens, slots), 0)
    taken = mask_here[...].astype(jnp.float32).T > 0.5
    valid = (positions < lengths_here[...].reshape(1, slots)) & (taken | (positions == 0))
    valid = wide(jnp.where(valid, 1.0, 0.0), 0.0)
    for i in range(parts):
        copies[i].wait()
        for p in range(i * each, (i + 1) * each):
            keep = jnp.broadcast_to(valid[:, p : p + 1], (tokens, LANES)).astype(jnp.bfloat16) > 0.5
            tok = out[p]
            out[p] = jnp.where(keep, tok, tok[0:1])


def fill(passages, lengths, mask):
    return pl.pallas_call(
        fill_kernel,
        out_shape=pltpu.VMEM(passages.shape, jnp.bfloat16),
        in_specs=[HBM] * 3,
        out_specs=VMEM,
        scratch_shapes=[
            pltpu.VMEM(mask.shape, jnp.int32),
            pltpu.VMEM(lengths.shape, jnp.int32),
            pltpu.SemaphoreType.DMA((10,)),
        ],
        compiler_params=params(16),
        cost_estimate=pl.CostEstimate(flops=0, bytes_accessed=passages.size * 4, transcendentals=0),
    )(*in_hbm(passages, lengths, mask))


def request_tables(blocks, me, block_rows, block_count, tokens, cand_count, slots):
    per_block = REQUEST_ROWS // 2
    queries = block_count * per_block
    target = []
    for b in range(block_count):
        first = b * block_rows + block_rows - REQUEST_ROWS
        request = blocks[first : first + REQUEST_ROWS, :].astype(jnp.float32)
        target.append(jnp.where(request[:per_block] == me, request[per_block:], -1.0))
    target = jnp.concatenate(target, axis=0)
    lane = lax.broadcasted_iota(jnp.int32, (queries, LANES), 1).astype(jnp.float32)
    named = jnp.zeros((queries, LANES), jnp.float32)
    for c in range(cand_count):
        named = jnp.where(target[:, c : c + 1] == lane, 1.0, named)
    row = lax.broadcasted_iota(jnp.int32, (queries, queries), 0)
    column = lax.broadcasted_iota(jnp.int32, (queries, queries), 1)
    earlier = (column < row).astype(jnp.bfloat16)
    rank = jnp.dot(earlier, named.astype(jnp.bfloat16), preferred_element_type=jnp.float32)
    rank = jnp.where(named > 0.5, rank, -1.0)
    number = lax.broadcasted_iota(jnp.int32, (queries, LANES), 0)
    place = lax.div(number, per_block) * block_rows + lax.rem(number, per_block) * tokens
    place = place.astype(jnp.float32)
    lists = [jnp.sum(jnp.where(rank == r, place, 0.0), axis=0, keepdims=True) for r in range(queries)]
    count = jnp.sum(named, axis=0, keepdims=True)
    return rank, jnp.concatenate(lists, axis=0).astype(jnp.int32), count


def overflow_list(count, slots, most):
    capacity = slots * (most - 1)
    later = jnp.maximum(jnp.floor((count + (GROUP - 1)) * (1.0 / GROUP)) - 1.0, 0.0)
    later = jnp.broadcast_to(later, (8, LANES))
    row = lax.broadcasted_iota(jnp.int32, (LANES, LANES), 0)
    column = lax.broadcasted_iota(jnp.int32, (LANES, LANES), 1)
    before = jnp.dot(later.astype(jnp.bfloat16), (row < column).astype(jnp.bfloat16), preferred_element_type=jnp.float32)
    entry = lax.broadcasted_iota(jnp.int32, (capacity, LANES), 0).astype(jnp.float32)
    mine = ((before[0:1] <= entry) & (entry < before[0:1] + later[0:1])).astype(jnp.bfloat16)
    passage = lax.broadcasted_iota(jnp.int32, (8, LANES), 1).astype(jnp.float32)
    kind = lax.broadcasted_iota(jnp.int32, (8, LANES), 0)
    facts = jnp.where(kind == 0, passage, jnp.where(kind == 1, before, later)).astype(jnp.bfloat16)
    found = lax.dot_general(facts, mine, NT, preferred_element_type=jnp.float32)
    total = jnp.sum(later[0:1], axis=1, keepdims=True)
    at = lax.broadcasted_iota(jnp.int32, (1, capacity), 1).astype(jnp.float32)
    group = jnp.clip(at - found[1:2] + 1.0, 1.0, float(most - 1))
    total = jnp.broadcast_to(total, (1, capacity))
    return jnp.concatenate([found[0:1], group, total], axis=0).astype(jnp.int32)


def token_means(best, tokens):
    columns = best.shape[1]
    row = lax.broadcasted_iota(jnp.int32, (GROUP, columns), 0)
    column = lax.broadcasted_iota(jnp.int32, (GROUP, columns), 1)
    pick = (row == lax.div(column, tokens)).astype(jnp.bfloat16)
    total = jnp.zeros((GROUP, best.shape[0]), jnp.float32)
    rest = best
    for _ in range(3):
        part = rest.astype(jnp.bfloat16)
        total = total + lax.dot_general(pick, part, NT, preferred_element_type=jnp.float32)
        rest = rest - part.astype(jnp.float32)
    return total * (1.0 / tokens)


def score_blocks(
    block_rows, block_count, extra, tokens, cand_count, me, passages, blocks,
    best, table, lists_here, lists, extras_here, extras, sems,
):
    slots, length, dim = passages.shape
    queries = block_count * (REQUEST_ROWS // 2)
    most = queries // GROUP
    rank, listed, count = request_tables(blocks, me, block_rows, block_count, tokens, cand_count, slots)
    capacity = slots * (most - 1)
    lists_here[...] = listed
    copies = [pltpu.make_async_copy(lists_here.at[pl.ds(0, GROUP)], lists.at[pl.ds(0, GROUP)], sems.at[0])]
    copies[0].start()
    if most > 1:
        later = pl.ds(GROUP, queries - GROUP)
        copies.append(pltpu.make_async_copy(lists_here.at[later], lists.at[later], sems.at[1]))
        extras_here[0:3, 0:capacity] = overflow_list(count, slots, most)
        copies.append(pltpu.make_async_copy(extras_here, extras, sems.at[2]))
        copies[1].start()
        copies[2].start()
    copies[0].wait()

    def group_best(p, first):
        rows = [blocks[pl.ds(pl.multiple_of(lists[first + k, p], 16), tokens), :] for k in range(GROUP)]
        similar = lax.dot_general(
            passages[p], jnp.concatenate(rows, axis=0), NT, preferred_element_type=jnp.float32
        )
        return jnp.max(similar, axis=0, keepdims=True)

    def extra_facts(e):
        live = e < extras[2, 0]
        return jnp.where(live, extras[0, e], -1), extras[0, e], extras[1, e]

    lane = lax.broadcasted_iota(jnp.int32, (GROUP, LANES), 1)
    for p in range(slots):
        if p == EARLY:
            for copy in copies[1:]:
                copy.wait()
        best[p : p + 1, :] = group_best(p, 0)
    if most > 1:
        facts = [extra_facts(e) for e in range(extra)]
        for e, (_, p, j) in enumerate(facts):
            best[slots + e : slots + e + 1, :] = group_best(p, j * GROUP)
    table[0:GROUP, 0:slots] = token_means(best[0:slots, :], tokens)
    means = token_means(best[slots:, :], tokens)
    if most > 1:
        for j in range(1, most):
            total = jnp.zeros((GROUP, LANES), jnp.float32)
            for e, (at, _, its) in enumerate(facts):
                total = jnp.where(lane == jnp.where(its == j, at, -1), means[:, e : e + 1], total)
            table[j * GROUP : (j + 1) * GROUP, :] = total

        def step(i, carry):
            where = [extra_facts(i * extra + u) for u in range(extra)]
            for u, (_, p, j) in enumerate(where):
                best[u : u + 1, :] = group_best(p, j * GROUP)
            means = token_means(best[0:extra, :], tokens)
            for u, (at, _, j) in enumerate(where):
                rows = pl.ds(pl.multiple_of(j * GROUP, GROUP), GROUP)
                table[rows, :] = jnp.where(lane == at, means[:, u : u + 1], table[rows, :])
            return carry

        lax.fori_loop(1, lax.div(extras[2, 0] + (extra - 1), extra), step, 0)
    result = jnp.zeros((queries, LANES), jnp.float32)
    for r in range(queries):
        result = jnp.where(rank == r, table[r : r + 1, :], result)
    return result


def score_scratch(slots, tokens, queries, extra):
    return [
        pltpu.VMEM((slots + extra, GROUP * tokens), jnp.float32),
        pltpu.VMEM((queries, LANES), jnp.float32),
        pltpu.VMEM((queries, LANES), jnp.int32),
        pltpu.SMEM((queries, LANES), jnp.int32),
        pltpu.VMEM((8, 256), jnp.int32),
        pltpu.SMEM((8, 256), jnp.int32),
        pltpu.SemaphoreType.DMA((3,)),
    ]


def cost(passages, queries):
    return pl.CostEstimate(
        flops=2 * passages.size * 256 * (queries // 4), bytes_accessed=passages.size * 2, transcendentals=0
    )


def score_kernel(block_rows, block_count, extra, tokens, cand_count, me, passages, blocks, out, *scratch):
    out[...] = score_blocks(
        block_rows, block_count, extra, tokens, cand_count, me[0].astype(jnp.float32), passages, blocks, *scratch
    )


def score(me, passages, blocks, block_rows, block_count, extra, tokens, cand_count):
    queries = block_count * (REQUEST_ROWS // 2)
    return pl.pallas_call(
        functools.partial(score_kernel, block_rows, block_count, extra, tokens, cand_count),
        out_shape=jax.ShapeDtypeStruct((queries, LANES), jnp.float32),
        in_specs=[pl.BlockSpec(memory_space=pltpu.SMEM), VMEM, VMEM],
        out_specs=VMEM,
        scratch_shapes=score_scratch(passages.shape[0], tokens, queries, extra),
        compiler_params=params(16),
        cost_estimate=cost(passages, queries),
    )(me, passages, blocks)


def last_kernel(
    homes, block_rows, block_count, extra, tokens, cand_count, me, passages, blocks, earlier, out, *scratch
):
    per_block = REQUEST_ROWS // 2
    result = score_blocks(
        block_rows, block_count, extra, tokens, cand_count, me[0].astype(jnp.float32), passages, blocks, *scratch
    )
    before = len(homes) - block_count
    for b, (step, side) in enumerate(homes):
        home = jnp.bitwise_xor(lax.rem(me[0] + (len(homes) - step), len(homes)), side)
        at = (b if b < before else b - before) * per_block
        out[home] = earlier[at : at + per_block, :] if b < before else result[at : at + per_block, :]


def score_last(me, passages, blocks, earlier, homes, block_rows, block_count, extra, tokens, cand_count):
    per_block = REQUEST_ROWS // 2
    return pl.pallas_call(
        functools.partial(last_kernel, homes, block_rows, block_count, extra, tokens, cand_count),
        out_shape=jax.ShapeDtypeStruct((len(homes), per_block, LANES), jnp.float32),
        in_specs=[pl.BlockSpec(memory_space=pltpu.SMEM), VMEM, VMEM, VMEM],
        out_specs=VMEM,
        scratch_shapes=score_scratch(passages.shape[0], tokens, block_count * per_block, extra),
        compiler_params=params(16),
        cost_estimate=cost(passages, block_count * per_block),
    )(me, passages, blocks, earlier)


def select_kernel(returned, owner, slot, out):
    count = owner.shape[1]
    own, at = wide(owner[...], -1), wide(slot[...], 0)
    total = jnp.zeros(own.shape, jnp.float32)
    for s in range(returned.shape[0]):
        total = jnp.where(own == s, jnp.take_along_axis(returned[s], at, axis=1, mode="promise_in_bounds"), total)
    out[...] = total[:, :count]


def select(returned, owner, slot):
    return pl.pallas_call(
        select_kernel,
        out_shape=jax.ShapeDtypeStruct(owner.shape, jnp.float32),
        in_specs=[VMEM] * 3,
        out_specs=VMEM,
        compiler_params=params(4),
    )(returned, owner, slot)


def local(queries, passages, lengths, token_mask, cand_owner, cand_slot):
    shard_count = lax.axis_size("shard")
    query_count, tokens, dim = queries.shape
    cand_count = cand_owner.shape[1]
    block = pack(queries.reshape(query_count * tokens, dim), cand_owner, cand_slot)
    block_rows = block.shape[0]
    filled = fill(passages, lengths, token_mask)
    me = lax.axis_index("shard").reshape(1)
    sizes = dict(block_rows=block_rows, tokens=tokens, cand_count=cand_count)
    if shard_count == 8:
        swap = lambda x, d: lax.ppermute(x, "shard", [(i, i ^ d) for i in range(shard_count)])
        turn = lambda x, d: lax.ppermute(x, "shard", [(i, (i + d) % shard_count) for i in range(shard_count)])
        near, far, mid = turn(block, 6), turn(block, 4), turn(block, 2)
        own = swap(block, 1)
        near, filled = lax.optimization_barrier((near, filled))
        first = swap(near, 1)
        far, mid, near = lax.optimization_barrier((far, mid, near))
        second = swap(jnp.concatenate([far, mid], axis=0), 1)
        early = jnp.concatenate([block, near, far, mid, own], axis=0)
        late = jnp.concatenate([first, second], axis=0)
        early_scores = score(me, filled, early, block_count=5, extra=24, **sizes)
        homes = ((0, 0), (6, 0), (4, 0), (2, 0), (0, 1), (6, 1), (4, 1), (2, 1))
        by_home = score_last(me, filled, late, early_scores, homes, block_count=3, extra=4, **sizes)
    else:
        every = lax.all_gather(block, "shard", axis=0, tiled=True)
        parts = every.reshape(shard_count // 4, 4 * block_rows, dim)
        by_home = lax.map(lambda part: score(me, filled, part, block_count=4, extra=12, **sizes), parts)
        by_home = by_home.reshape(shard_count, query_count, LANES)
    returned = lax.all_to_all(by_home, "shard", split_axis=0, concat_axis=0, tiled=True)
    return select(returned, cand_owner, cand_slot)


def solution(mesh):
    in_specs = (
        P(("groups", "shard", "rep"), None, None),
        P(("groups", "shard"), None, None),
        P(("groups", "shard")),
        P(("groups", "shard"), None),
        P(("groups", "shard", "rep"), None),
        P(("groups", "shard", "rep"), None),
    )
    out_specs = P(("groups", "shard", "rep"), None)
    return jax.shard_map(local, mesh=mesh, in_specs=in_specs, out_specs=out_specs, check_vma=False)
```
